32 devices in a mesh: dp: 8 (over y, x, core), tensor: 4 (over z).
Axes of the slice: x: 2, y: 2, z: 4, core: 2. Of those that a mesh axis runs over, the one named last changes fastest.
Arguments:
- inputs: float32 [16384, 1024], P(('dp', 'tensor')), may hold values from -6 to 6
- lengths: int32 [8, 4], P('dp'), may hold values from 0 to 2048, as said below
- ln_gain: float32 [2, 2, 1024], replicated, may hold values from 0.1 to 1.9
- ln_bias: float32 [2, 2, 1024], replicated, may hold values from -4 to 4
- out_bias: float32 [2, 2, 1024], replicated, may hold values from -6 to 6
- w_qkv: bfloat16 [2, 1024, 3, 1024], P(None, None, None, 'tensor'), may hold values from -0.1875 to 0.1875
- qv_bias: float32 [2, 2, 1024], P(None, None, 'tensor'), may hold values from -6 to 6
- w_out: bfloat16 [2, 1024, 1024], P(None, 'tensor'), may hold values from -2 to 2
- w_in: bfloat16 [2, 1024, 4096], P(None, None, 'tensor'), may hold values from -0.1875 to 0.1875
- in_bias: float32 [2, 4096], P(None, 'tensor'), may hold values from -6 to 6
- w_down: bfloat16 [2, 4096, 1024], P(None, 'tensor'), may hold values from -0.09375 to 0.09375
- out_grad: float32 [16384, 1024], P(('dp', 'tensor')), may hold values from -6 to 6
Outputs:
- outputs: float32 [16384, 1024], P(('dp', 'tensor'))
- input_grad: float32 [16384, 1024], P(('dp', 'tensor'))
- grad_ln_gain: float32 [2, 2, 1024], P(None, None, ('dp', 'tensor'))
- grad_ln_bias: float32 [2, 2, 1024], P(None, None, ('dp', 'tensor'))
- grad_out_bias: float32 [2, 2, 1024], P(None, None, ('dp', 'tensor'))
- grad_w_qkv: float32 [2, 1024, 3, 1024], P(None, 'dp', None, 'tensor')
- grad_qv_bias: float32 [2, 2, 1024], P(None, None, ('tensor', 'dp'))
- grad_w_out: float32 [2, 1024, 1024], P(None, 'tensor', 'dp')
- grad_w_in: float32 [2, 1024, 4096], P(None, 'dp', 'tensor')
- grad_in_bias: float32 [2, 4096], P(None, ('tensor', 'dp'))
- grad_w_down: float32 [2, 4096, 1024], P(None, 'tensor', 'dp')
The draws below stay inside these ranges and needn't reach their ends.
Inputs may be any that keep to these rules, and one draw needn't show every extreme that they name: In each group the 4 lengths sum to 2048, and the group's documents lie in its rows in the order of its lengths; some lengths are zero.
All inputs are finite; a program needn't handle non-finite values.
Results may differ from the reference program's by a relative error of at most 0.02.
Values may be sent and summed in bfloat16 or wider, within the bound.
A program may use at most 320 MiB of HBM per device.

```python
import jax
import jax.numpy as jnp
from jax import lax

D = 1024
HEADS = 8
HEAD = 128
FF = 4096
LAYERS = 2
SEQS = 4
TOK_DEV = 2048
TOKENS = 16384
N_DP = 8
N_TENSOR = 4


def draw_lengths(key, part):
    key = jax.random.fold_in(key, 11)
    dev_rows = TOK_DEV // N_TENSOR
    short_cap = (dev_rows - 1) // 3
    key_short, key_group, key_slot = jax.random.split(key, 3)
    shorts = jax.random.randint(key_short, (N_DP, SEQS - 1), 0, short_cap + 1).astype(jnp.int32)
    whole_group = jax.random.randint(key_group, (), 0, N_DP).astype(jnp.int32)
    group_ids = jnp.arange(N_DP, dtype=jnp.int32)[:, None]
    shorts = jnp.where(group_ids == whole_group, 0, shorts).astype(jnp.int32)
    long_slot = jax.random.randint(key_slot, (N_DP, 1), 0, SEQS).astype(jnp.int32)
    longest = (TOK_DEV - jnp.sum(shorts, 1, keepdims=True)).astype(jnp.int32)
    blank = jnp.zeros((N_DP, 1), jnp.int32)
    left_side = jnp.concatenate([shorts, blank], 1)
    right_side = jnp.concatenate([blank, shorts], 1)
    slot_ids = jnp.arange(SEQS, dtype=jnp.int32)[None, :]
    chosen = jnp.where(slot_ids < long_slot, left_side, jnp.where(slot_ids == long_slot, longest, right_side))
    return chosen.astype(jnp.int32)


def levels(stream_key, dims, cuts, least, high):
    factor_of = 1.0
    for dim, parts in cuts:
        steps = jax.random.uniform(jax.random.fold_in(jax.random.fold_in(stream_key, 6), dim), (parts,), jnp.float32, least / len(cuts), high / len(cuts))
        factor_of = factor_of * jnp.repeat(jnp.exp(steps), dims[dim] // parts).reshape((-1,) + (1,) * (len(dims) - 1 - dim))
    return factor_of


def bell_draw(own_key, dims, scale, bound, shards=(), held_as=jnp.bfloat16):
    drawn = jax.random.normal(own_key, dims, jnp.float32) * scale
    if len(shards) > 0:
        drawn = levels(own_key, dims, shards, -0.22, 0.18) * drawn
    return jnp.clip(drawn, min=-bound, max=bound).astype(held_as)


def setup_inputs(seed: int = 0) -> dict:
    keys = jax.random.split(jax.random.key(seed), 13)
    return {
        "inputs": bell_draw(keys[0], (TOKENS, D), 1.0, 6.0, ((0, 32),), jnp.float32),
        "lengths": draw_lengths(jax.random.fold_in(keys[12], 71), 0),
        "ln_gain": jnp.clip(1.0 + 0.18 * jax.random.normal(keys[2], (LAYERS, 2, D), jnp.float32), 0.1, 1.9),
        "ln_bias": bell_draw(keys[3], (LAYERS, 2, D), 0.3, 4.0, (), jnp.float32),
        "out_bias": bell_draw(keys[4], (LAYERS, 2, D), 0.5, 6.0, (), jnp.float32),
        "w_qkv": bell_draw(keys[5], (LAYERS, D, 3, HEADS * HEAD), D ** -0.5, 0.1875, ((3, 4),)),
        "qv_bias": bell_draw(keys[6], (LAYERS, 2, HEADS * HEAD), 0.5, 6.0, ((2, 4),), jnp.float32),
        "w_out": bell_draw(keys[7], (LAYERS, HEADS * HEAD, D), (max(D * 16 // TOK_DEV, 4)) ** -0.5, 2.0, ((1, 4),)),
        "w_in": bell_draw(keys[8], (LAYERS, D, FF), D ** -0.5, 0.1875, ((2, 4),)),
        "in_bias": bell_draw(keys[9], (LAYERS, FF), 0.5, 6.0, ((1, 4),), jnp.float32),
        "w_down": bell_draw(keys[10], (LAYERS, FF, D), FF ** -0.5, 0.09375, ((1, 4),)),
        "out_grad": bell_draw(keys[11], (TOKENS, D), 1.0, 6.0, ((0, 32),), jnp.float32),
    }


EPS = 1e-05
NEG = -1e+30
HIGH = lax.Precision.HIGHEST

@jax.custom_vjp
def low(v):
    return lax.optimization_barrier(v.astype(jnp.bfloat16)).astype(jnp.float32)

@jax.custom_vjp
def low_back(v):
    return v

def low_keep(v):
    return (low(v), None)

def low_pass(kept, grad):
    return (grad,)

def back_keep(v):
    return (v, None)

def back_low(kept, grad):
    return (low(grad),)
low.defvjp(low_keep, low_pass)
low_back.defvjp(back_keep, back_low)

def layer_norm(values, gain_vec, bias_vec):
    centre = values - lax.optimization_barrier(jnp.mean(values, -1, keepdims=True))
    spread = lax.optimization_barrier(jnp.mean(centre * centre, -1, keepdims=True))
    return centre * lax.rsqrt(spread + EPS) * gain_vec + bias_vec

def matmul_hi(left, right):
    return jnp.dot(left, right, precision=HIGH, preferred_element_type=jnp.float32)

def segment_ids(lengths_row, tokens):
    doc_ends = jnp.cumsum(lengths_row.astype(jnp.int32)).astype(jnp.int32)
    positions = jnp.arange(tokens, dtype=jnp.int32)
    return lax.optimization_barrier(jnp.sum((positions[:, None] >= doc_ends[None, :]).astype(jnp.int32), 1)).astype(jnp.int32)

def attend(queries, key_rows, value_rows, seg_ids):
    tokens = queries.shape[0]
    block_len = min(512, tokens)
    positions = jnp.arange(tokens, dtype=jnp.int32)
    score_scale = float(HEAD) ** (-0.5)

    def one_block(block_id):
        row_start = (block_id * block_len).astype(jnp.int32)
        q_rows = lax.dynamic_slice_in_dim(queries, row_start, block_len, 0)
        row_ids = row_start + jnp.arange(block_len, dtype=jnp.int32)
        row_segs = lax.dynamic_slice_in_dim(seg_ids, row_start, block_len, 0)
        scores = low_back(jnp.einsum('qhd,khd->hqk', q_rows, key_rows, precision=HIGH)) * score_scale
        allowed = (row_segs[:, None] == seg_ids[None, :]) & (positions[None, :] <= row_ids[:, None])
        scores = jnp.where(allowed[None], scores, NEG)
        weights = low(jax.nn.softmax(scores, -1))
        return jnp.einsum('hqk,khd->qhd', weights, value_rows, precision=HIGH)
    blocks = lax.map(jax.checkpoint(one_block), jnp.arange(tokens // block_len, dtype=jnp.int32))
    return blocks.reshape(tokens, HEADS * HEAD)

def forward(stream, seg_ids, ln_gain, ln_bias, out_bias, w_qkv, qv_bias, w_out, w_in, in_bias, w_down):
    inner_width = HEADS * HEAD
    head_shape = (stream.shape[0], HEADS, HEAD)
    for layer_id in range(LAYERS):
        normed = low(layer_norm(stream, ln_gain[layer_id, 0], ln_bias[layer_id, 0]))
        projected = matmul_hi(normed, w_qkv[layer_id].reshape(D, 3 * inner_width))
        queries = low_back(low(projected[:, :inner_width] + qv_bias[layer_id, 0]))
        key_rows = low_back(low(projected[:, inner_width:2 * inner_width]))
        value_rows = low_back(low(projected[:, 2 * inner_width:] + qv_bias[layer_id, 1]))
        attended = low_back(low(attend(queries.reshape(head_shape), key_rows.reshape(head_shape), value_rows.reshape(head_shape), seg_ids)))
        stream = stream + low_back(matmul_hi(attended, w_out[layer_id])) + out_bias[layer_id, 0]
        normed = low(layer_norm(stream, ln_gain[layer_id, 1], ln_bias[layer_id, 1]))
        hidden = low_back(matmul_hi(normed, w_in[layer_id]) + in_bias[layer_id])
        active = low(jax.nn.gelu(hidden))
        stream = stream + low_back(matmul_hi(active, w_down[layer_id])) + out_bias[layer_id, 1]
    return stream

def reference(inputs, lengths, ln_gain, ln_bias, out_bias, w_qkv, qv_bias, w_out, w_in, in_bias, w_down, out_grad):
    params = (ln_gain, ln_bias, out_bias, w_qkv.astype(jnp.float32), qv_bias, w_out.astype(jnp.float32), w_in.astype(jnp.float32), in_bias, w_down.astype(jnp.float32))
    grouped = inputs.reshape(N_DP, TOK_DEV, D)
    cotangent = out_grad.reshape(N_DP, TOK_DEV, D)

    def group_step(totals, group_item):
        rows_in, lengths_row, rows_grad = group_item
        seg_ids = segment_ids(lengths_row, TOK_DEV)

        def group_forward(stream, *weights):
            return forward(stream, seg_ids, *weights)
        result, pullback = jax.vjp(group_forward, rows_in, *params)
        gradients = pullback(rows_grad)
        totals = tuple((total_item + grad_item for total_item, grad_item in zip(totals, gradients[1:])))
        return (totals, (result, gradients[0]))
    initial = tuple((jnp.zeros(param.shape, jnp.float32) for param in params))
    totals, (results, input_grads) = lax.scan(group_step, initial, (grouped, lengths, cotangent))
    return (results.reshape(TOKENS, D), input_grads.reshape(TOKENS, D), totals[0], totals[1], totals[2], totals[3], totals[4], totals[5], totals[6], totals[7], totals[8])
```

```python
import functools

import jax
import jax.numpy as jnp
from jax import lax
from jax.experimental import pallas as pl
from jax.experimental.pallas import tpu as pltpu
from jax.sharding import PartitionSpec as P

D = 1024
HEAD = 128
LAYERS = 2
LOG2E = 1.4426950408889634
VMEM_LIMIT = 56 * 1024 * 1024


EPS = 1e-05
NEG = -1e30


def layer_norm(values, gain_vec, bias_vec):
    centre = values - jnp.mean(values, -1, keepdims=True)
    spread = jnp.mean(centre * centre, -1, keepdims=True)
    return centre * lax.rsqrt(spread + EPS) * gain_vec + bias_vec


def contract_rows(left, right):
    return lax.dot_general(
        left, right, (((0,), (0,)), ((), ())), preferred_element_type=jnp.float32
    )


def contract_cols(left, right):
    return lax.dot_general(
        left, right, (((1,), (1,)), ((), ())), preferred_element_type=jnp.float32
    )


def doc_starts(lengths_row, tokens):
    doc_ends = jnp.cumsum(lengths_row)
    positions = jnp.arange(tokens, dtype=jnp.int32)
    return jnp.max(jnp.where(positions[:, None] >= doc_ends[None, :], doc_ends[None, :], 0), 1)[None]

def dot_nt(a,b):
    return lax.dot_general(a,b,(((1,),(1,)),((),())),preferred_element_type=jnp.float32)
def dot_nn(a,b):
    return lax.dot_general(a,b,(((1,),(0,)),((),())),preferred_element_type=jnp.float32)

def attn_fwd_kernel(block, starts_ref, q_ref, k_ref, v_ref, o_ref, p_ref, s_scr):
    tokens=q_ref.shape[0]
    factor=float(HEAD)**-0.5*LOG2E
    vt=v_ref[...].T
    for i in range(tokens//block):
        qi=q_ref[i*block:(i+1)*block,:]
        start_row=starts_ref[0:1,i*block:(i+1)*block]
        base=i*(i+1)//2*block
        peak=None
        for j in range(i+1):
            s=dot_nt(k_ref[j*block:(j+1)*block,:],qi)*factor
            key_ids=j*block+lax.broadcasted_iota(jnp.int32,(block,block),0)
            ok=key_ids>=start_row
            if j==i:
                ok=ok&(key_ids<=i*block+lax.broadcasted_iota(jnp.int32,(block,block),1))
            s=jnp.where(ok,s,NEG)
            s_scr[j*block:(j+1)*block,:]=s
            top=jnp.max(s,0,keepdims=True)
            peak=top if peak is None else jnp.maximum(peak,top)
        total=None
        for j in range(i+1):
            e=jnp.exp2(s_scr[j*block:(j+1)*block,:]-peak)
            s_scr[j*block:(j+1)*block,:]=e
            part=jnp.sum(e,0,keepdims=True)
            total=part if total is None else total+part
        inv=1.0/total
        acc=None
        for j in range(i+1):
            p=(s_scr[j*block:(j+1)*block,:]*inv).astype(jnp.bfloat16)
            p_ref[0,base+j*block:base+(j+1)*block,:]=p
            part=dot_nn(vt[:,j*block:(j+1)*block],p)
            acc=part if acc is None else acc+part
        o_ref[i*block:(i+1)*block,:]=acc.T.astype(jnp.bfloat16)

def attn_fwd(q,k,v,starts):
    tokens,inner=q.shape
    heads=inner//HEAD
    block=min(512,tokens)
    nb=tokens//block
    packed=nb*(nb+1)//2*block
    spec=pl.BlockSpec((tokens,HEAD),lambda h:(0,h))
    return pl.pallas_call(
        functools.partial(attn_fwd_kernel,block),
        grid=(heads,),
        in_specs=[pl.BlockSpec((1,tokens),lambda h:(0,0)),spec,spec,spec],
        out_specs=[spec,pl.BlockSpec((1,packed,block),lambda h:(h,0,0))],
        out_shape=[jax.ShapeDtypeStruct((tokens,inner),jnp.bfloat16),jax.ShapeDtypeStruct((heads,packed,block),jnp.bfloat16)],
        scratch_shapes=[pltpu.VMEM((tokens,block),jnp.float32)],
        compiler_params=pltpu.CompilerParams(vmem_limit_bytes=VMEM_LIMIT),
    )(starts,q,k,v)

def attn_bwd_kernel(block,q_ref,k_ref,v_ref,o_ref,do_ref,p_ref,dq_ref,dk_ref,dv_ref,dk_acc,dv_acc):
    tokens=q_ref.shape[0]
    scale=float(HEAD)**-0.5
    kt=k_ref[...].T
    for i in range(tokens//block):
        rows=slice(i*block,(i+1)*block)
        qi=q_ref[rows,:]
        doi=do_ref[rows,:]
        prod=doi.astype(jnp.float32)*o_ref[rows,:].astype(jnp.float32)
        inner=jnp.sum(prod.T,0,keepdims=True)
        base=i*(i+1)//2*block
        acc=None
        for j in range(i+1):
            cols=slice(j*block,(j+1)*block)
            p=p_ref[0,base+j*block:base+(j+1)*block,:]
            dp=dot_nt(v_ref[cols,:],doi)
            ds=(p.astype(jnp.float32)*(dp-inner)).astype(jnp.bfloat16)
            dv=dot_nn(p,doi)
            dk=dot_nn(ds,qi)
            if i==j:
                dv_acc[cols,:]=dv
                dk_acc[cols,:]=dk
            else:
                dv_acc[cols,:]+=dv
                dk_acc[cols,:]+=dk
            part=dot_nn(kt[:,cols],ds)
            acc=part if acc is None else acc+part
        dq_ref[rows,:]=(acc*scale).T.astype(jnp.bfloat16)
    dk_ref[...]=(dk_acc[...]*scale).astype(jnp.bfloat16)
    dv_ref[...]=dv_acc[...].astype(jnp.bfloat16)

def attn_bwd(q,k,v,o,do,p):
    tokens,inner=q.shape
    heads=inner//HEAD
    block=min(512,tokens)
    packed=p.shape[1]
    spec=pl.BlockSpec((tokens,HEAD),lambda h:(0,h))
    shape=jax.ShapeDtypeStruct((tokens,inner),jnp.bfloat16)
    return pl.pallas_call(
        functools.partial(attn_bwd_kernel,block),
        grid=(heads,),
        in_specs=[spec]*5+[pl.BlockSpec((1,packed,block),lambda h:(h,0,0))],
        out_specs=[spec]*3,
        out_shape=[shape]*3,
        scratch_shapes=[pltpu.VMEM((tokens,HEAD),jnp.float32)]*2,
        compiler_params=pltpu.CompilerParams(vmem_limit_bytes=VMEM_LIMIT),
    )(q,k,v,o,do,p)


def gather_normed(normed):
    return lax.all_gather(normed, "tensor", axis=0, tiled=True)


def feed_sum(active, weight):
    return lax.psum_scatter(
        jnp.dot(active, weight, preferred_element_type=jnp.float32).astype(jnp.bfloat16),
        "tensor",
        scatter_dimension=0,
        tiled=True,
    ).astype(jnp.float32)


def input_sum(grads, weight):
    return lax.psum_scatter(
        contract_cols(grads, weight).astype(jnp.bfloat16), "tensor", scatter_dimension=0, tiled=True
    ).astype(jnp.float32)


def on_device(
    inputs,
    lengths,
    ln_gain,
    ln_bias,
    out_bias,
    w_qkv,
    qv_bias,
    w_out,
    w_in,
    in_bias,
    w_down,
    out_grad,
):
    dev_rows = inputs.shape[0]
    tokens = dev_rows * lax.axis_size("tensor")
    inner = qv_bias.shape[2]
    starts = doc_starts(lengths[0], tokens)
    stream = inputs
    kept = []
    for layer_id in range(LAYERS):
        normed = layer_norm(stream, ln_gain[layer_id, 0], ln_bias[layer_id, 0]).astype(jnp.bfloat16)
        full_one = gather_normed(normed)
        projected = jnp.dot(
            full_one, w_qkv[layer_id].reshape(D, 3 * inner), preferred_element_type=jnp.float32
        )
        queries = (projected[:, :inner] + qv_bias[layer_id, 0]).astype(jnp.bfloat16)
        key_rows = projected[:, inner : 2 * inner].astype(jnp.bfloat16)
        value_rows = (projected[:, 2 * inner :] + qv_bias[layer_id, 1]).astype(jnp.bfloat16)
        attended, probs = attn_fwd(queries, key_rows, value_rows, starts)
        out_full = lax.all_gather(w_out[layer_id], "tensor", axis=0, tiled=True)
        head_rows = lax.all_to_all(attended, "tensor", split_axis=0, concat_axis=1, tiled=True)
        branch = jnp.dot(head_rows, out_full, preferred_element_type=jnp.float32)
        middle = stream + branch + out_bias[layer_id, 0]
        normed_two = layer_norm(middle, ln_gain[layer_id, 1], ln_bias[layer_id, 1]).astype(
            jnp.bfloat16
        )
        full_two = gather_normed(normed_two)
        hidden = (
            jnp.dot(full_two, w_in[layer_id], preferred_element_type=jnp.float32)
            + in_bias[layer_id]
        )
        active = jax.nn.gelu(hidden).astype(jnp.bfloat16)
        kept.append(
            (
                stream,
                full_one,
                queries,
                key_rows,
                value_rows,
                probs,
                attended,
                head_rows,
                out_full,
                middle,
                full_two,
                hidden,
                active,
            )
        )
        stream = middle + feed_sum(active, w_down[layer_id]) + out_bias[layer_id, 1]
    grad = out_grad
    per_layer = [None] * LAYERS
    for layer_id in reversed(range(LAYERS)):
        (
            entry,
            full_one,
            queries,
            key_rows,
            value_rows,
            probs,
            attended,
            head_rows,
            out_full,
            middle,
            full_two,
            hidden,
            active,
        ) = kept[layer_id]
        bias_two = jnp.sum(grad, 0)
        grad_low = grad.astype(jnp.bfloat16)
        grad_full = lax.all_gather(grad_low, "tensor", axis=0, tiled=True)
        grad_down = contract_rows(active, grad_full)
        grad_active = contract_cols(grad_full, w_down[layer_id])
        gelu_value, gelu_pull = jax.vjp(jax.nn.gelu, hidden)
        grad_hidden = gelu_pull(grad_active)[0].astype(jnp.bfloat16)
        bias_in = jnp.sum(grad_hidden, 0, dtype=jnp.float32)
        grad_up = contract_rows(full_two, grad_hidden)
        grad_normed = input_sum(grad_hidden, w_in[layer_id])
        norm_value, norm_pull = jax.vjp(
            layer_norm, middle, ln_gain[layer_id, 1], ln_bias[layer_id, 1]
        )
        grad_middle, gain_two, shift_two = norm_pull(grad_normed)
        grad = grad + grad_middle
        bias_one = jnp.sum(grad, 0)
        grad_mid_low = grad.astype(jnp.bfloat16)
        grad_proj_w = lax.psum_scatter(
            contract_rows(head_rows, grad_mid_low).astype(jnp.bfloat16),
            "tensor",
            scatter_dimension=0,
            tiled=True,
        ).astype(jnp.float32)
        grad_heads = contract_cols(grad_mid_low, out_full).astype(jnp.bfloat16)
        grad_attended = lax.all_to_all(
            grad_heads, "tensor", split_axis=1, concat_axis=0, tiled=True
        )
        low_q, low_k, low_v = attn_bwd(
            queries, key_rows, value_rows, attended, grad_attended, probs
        )
        grad_mixed = jnp.concatenate([low_q, low_k, low_v], 1)
        grad_qkv_w = contract_rows(full_one, grad_mixed).reshape(D, 3, inner)
        grad_qv = jnp.stack(
            [jnp.sum(low_q, 0, dtype=jnp.float32), jnp.sum(low_v, 0, dtype=jnp.float32)]
        )
        grad_normed_one = input_sum(grad_mixed, w_qkv[layer_id].reshape(D, 3 * inner))
        norm_value, norm_pull = jax.vjp(
            layer_norm, entry, ln_gain[layer_id, 0], ln_bias[layer_id, 0]
        )
        grad_entry, gain_one, shift_one = norm_pull(grad_normed_one)
        grad = grad + grad_entry
        per_layer[layer_id] = (
            jnp.stack([gain_one, gain_two]),
            jnp.stack([shift_one, shift_two]),
            jnp.stack([bias_one, bias_two]),
            grad_qkv_w,
            grad_qv,
            grad_proj_w,
            grad_up,
            bias_in,
            grad_down,
        )
    gain_all = jnp.stack([entry_grads[0] for entry_grads in per_layer])
    shift_all = jnp.stack([entry_grads[1] for entry_grads in per_layer])
    outb_all = jnp.stack([entry_grads[2] for entry_grads in per_layer])
    qkv_all = jnp.stack([entry_grads[3] for entry_grads in per_layer])
    qvb_all = jnp.stack([entry_grads[4] for entry_grads in per_layer])
    proj_all = jnp.stack([entry_grads[5] for entry_grads in per_layer])
    up_all = jnp.stack([entry_grads[6] for entry_grads in per_layer])
    inb_all = jnp.stack([entry_grads[7] for entry_grads in per_layer])
    down_all = jnp.stack([entry_grads[8] for entry_grads in per_layer])
    qkv_sum, qvb_sum, proj_sum, up_sum, inb_sum, down_sum = (
        lax.psum_scatter(
            qkv_all.astype(jnp.bfloat16), "dp", scatter_dimension=1, tiled=True
        ).astype(jnp.float32),
        lax.psum_scatter(
            qvb_all.astype(jnp.bfloat16), "dp", scatter_dimension=2, tiled=True
        ).astype(jnp.float32),
        lax.psum_scatter(
            proj_all.astype(jnp.bfloat16), "dp", scatter_dimension=2, tiled=True
        ).astype(jnp.float32),
        lax.psum_scatter(up_all.astype(jnp.bfloat16), "dp", scatter_dimension=1, tiled=True).astype(
            jnp.float32
        ),
        lax.psum_scatter(
            inb_all.astype(jnp.bfloat16), "dp", scatter_dimension=1, tiled=True
        ).astype(jnp.float32),
        lax.psum_scatter(
            down_all.astype(jnp.bfloat16), "dp", scatter_dimension=2, tiled=True
        ).astype(jnp.float32),
    )
    gain_sum, shift_sum, outb_sum = (
        lax.psum_scatter(gain_all, ("dp", "tensor"), scatter_dimension=2, tiled=True),
        lax.psum_scatter(shift_all, ("dp", "tensor"), scatter_dimension=2, tiled=True),
        lax.psum_scatter(outb_all, ("dp", "tensor"), scatter_dimension=2, tiled=True),
    )
    return (
        stream,
        grad,
        gain_sum,
        shift_sum,
        outb_sum,
        qkv_sum,
        qvb_sum,
        proj_sum,
        up_sum,
        inb_sum,
        down_sum,
    )


def solution(mesh):
    return jax.shard_map(
        on_device,
        mesh=mesh,
        in_specs=(
            P(("dp", "tensor"), None),
            P("dp", None),
            P(),
            P(),
            P(),
            P(None, None, None, "tensor"),
            P(None, None, "tensor"),
            P(None, "tensor", None),
            P(None, None, "tensor"),
            P(None, "tensor"),
            P(None, "tensor", None),
            P(("dp", "tensor"), None),
        ),
        out_specs=(
            P(("dp", "tensor"), None),
            P(("dp", "tensor"), None),
            P(None, None, ("dp", "tensor")),
            P(None, None, ("dp", "tensor")),
            P(None, None, ("dp", "tensor")),
            P(None, "dp", None, "tensor"),
            P(None, None, ("tensor", "dp")),
            P(None, "tensor", "dp"),
            P(None, "dp", "tensor"),
            P(None, ("tensor", "dp")),
            P(None, "tensor", "dp"),
        ),
        check_vma=False,
    )
```
